32 devices in a mesh: fsdp: 32 (over z, y, x, core).
Axes of the slice: x: 2, y: 2, z: 4, core: 2. Of those that a mesh axis runs over, the one named last changes fastest.
Arguments:
- tokens: bfloat16 [32768, 768], P('fsdp'), may hold values from -6 to 6
- cotangent: bfloat16 [32768, 768], P('fsdp'), may hold values from -6 to 6
- lengths: int32 [64, 3], P('fsdp'), may hold values from 1 to 384, 512 in all within a row
- w_qkv: float32 [768, 2304], P('fsdp'), may hold values from -0.21875 to 0.21875
- w_out: float32 [768, 768], P('fsdp'), may hold values from -1.25 to 1.25
- w_fc: float32 [768, 3072], P('fsdp'), may hold values from -0.21875 to 0.21875
- w_proj: float32 [3072, 768], P('fsdp'), may hold values from -0.109375 to 0.109375
- vectors: float32 [9216], P('fsdp'), may hold values from -0.6 to 3.5
- m_qkv: float32 [768, 2304], P('fsdp'), may hold values from -0.00016527923 to 0.00016527923
- m_out: float32 [768, 768], P('fsdp'), may hold values from -0.00016527923 to 0.00016527923
- m_fc: float32 [768, 3072], P('fsdp'), may hold values from -0.00016527923 to 0.00016527923
- m_proj: float32 [3072, 768], P('fsdp'), may hold values from -0.00016527923 to 0.00016527923
- m_vectors: float32 [9216], P('fsdp'), may hold values from -0.00016527923 to 0.00016527923
- s_qkv: float32 [768, 2304], P('fsdp'), may hold values from 1.4110135e-10 to 5.644054e-10
- s_out: float32 [768, 768], P('fsdp'), may hold values from 1.4110135e-10 to 5.644054e-10
- s_fc: float32 [768, 3072], P('fsdp'), may hold values from 1.4110135e-10 to 5.644054e-10
- s_proj: float32 [3072, 768], P('fsdp'), may hold values from 1.4110135e-10 to 5.644054e-10
- s_vectors: float32 [9216], P('fsdp'), may hold values from 1.4110135e-10 to 5.644054e-10
Outputs:
- output: bfloat16 [32768, 768], P('fsdp')
- input_grad: float32 [32768, 768], P('fsdp')
- grad_norm: float32 [], replicated
- new_qkv: float32 [768, 2304], P('fsdp')
- new_out: float32 [768, 768], P('fsdp')
- new_fc: float32 [768, 3072], P('fsdp')
- new_proj: float32 [3072, 768], P('fsdp')
- new_vectors: float32 [9216], P('fsdp')
- first_qkv: float32 [768, 2304], P('fsdp')
- first_out: float32 [768, 768], P('fsdp')
- first_fc: float32 [768, 3072], P('fsdp')
- first_proj: float32 [3072, 768], P('fsdp')
- first_vectors: float32 [9216], P('fsdp')
- second_qkv: float32 [768, 2304], P('fsdp')
- second_out: float32 [768, 768], P('fsdp')
- second_fc: float32 [768, 3072], P('fsdp')
- second_proj: float32 [3072, 768], P('fsdp')
- second_vectors: float32 [9216], P('fsdp')
The draws below stay inside these ranges and needn't reach their ends.
Inputs may be any that keep to these rules, and one draw needn't show every extreme that they name: Each row's 3 lengths sum to 512, and the largest of each row is 384.
All inputs are finite; a program needn't handle non-finite values.
Results may differ from the reference program's by a relative error of at most 0.0095.
The reference program's roundings to bfloat16 on the way count: a program that leaves them out, or rounds other values in their place, can miss the bound.
Values may be sent and summed in bfloat16 or wider, within the bound.
A program may use at most 192 MiB of HBM per device.

```python
import math
import jax
import jax.numpy as jnp
import numpy as np
from jax import lax

D = 768
H = 12
HD = 64
FF = 3072
S = 512
SEQS = 3
STEP = 10
MOST = 384
MICRO = 64
TOKENS = 32768
PARAMS = 7087104
NVEC = 9216


def draw_vectors(key, part):
    key = jax.random.fold_in(key, 11)
    key_gain, key_shift = jax.random.split(key)
    placing = jnp.arange(D, dtype=jnp.float32) / (D - 1)
    ramp = 0.6 + 1.2 * placing
    wobble = jax.random.uniform(key_gain, (2, D), jnp.float32, 0.8, 1.25)
    shifts = 0.2 * jnp.clip(jax.random.normal(key_shift, (6 * D + FF,), jnp.float32), -3.0, 3.0)
    gains = ramp[None, :] * wobble
    return jnp.concatenate([gains[0], shifts[0:D], shifts[D:2 * D], shifts[2 * D:3 * D], shifts[3 * D:4 * D], gains[1], shifts[4 * D:5 * D], shifts[5 * D:6 * D], shifts[6 * D:]]).astype(jnp.float32)


def block_scale(own_key, dims, shards, least, largest):
    factor_of = 1.0
    for axis_at, parts in shards:
        draws = jax.random.uniform(jax.random.fold_in(jax.random.fold_in(own_key, 6), axis_at), (parts,), jnp.float32, least / len(shards), largest / len(shards))
        factor_of = factor_of * jnp.repeat(jnp.exp(draws), dims[axis_at] // parts).reshape((-1,) + (1,) * (len(dims) - 1 - axis_at))
    return factor_of


def split_up(amount, total, limit, slope):
    portions = [(1 << 20) // math.isqrt(rank ** slope) + 1 for rank in range(2, amount + 1)]
    rest, given = total - limit - (amount - 1), [1] * (amount - 1)
    while rest > 0:
        free = [i for i in range(amount - 1) if given[i] < limit]
        pool, budget = sum([portions[i] for i in free]), rest
        for i in free:
            extra = min(limit - given[i], max(1, budget * portions[i] // pool), rest)
            given[i] = given[i] + extra
            rest = rest - extra
    return np.array([limit] + given)


def uneven_parts(key, count, total, limit, skew):
    if count == 2:
        one = jax.random.randint(key, (), max(1, total - limit), min(limit, total - 1) + 1)
        return jnp.stack([one, total - one])
    tallies = jnp.asarray(split_up(count, total, limit, skew), jnp.int32)
    couples = (count - 1) // 2
    source_of, taker = tallies[1:1 + 2 * couples:2], tallies[2:2 + 2 * couples:2]
    slack = jnp.minimum(source_of - 1, limit - taker)
    passed = jax.random.randint(jax.random.fold_in(key, 1), (couples,), 0, 1 << 20) % (slack + 1)
    tallies = tallies.at[1:1 + 2 * couples:2].set(source_of - passed).at[2:2 + 2 * couples:2].set(taker + passed)
    return tallies[jax.random.permutation(jax.random.fold_in(key, 2), count)]


def normal_values(key, dims, spread, reach, cuts=(), kind=jnp.bfloat16):
    loudness = block_scale(key, dims, cuts, -0.22, 0.18) if cuts else 1.0
    entries = jax.random.normal(key, dims, jnp.float32) * spread * loudness
    return jnp.minimum(jnp.maximum(entries, -reach), reach).astype(kind)


def setup_inputs(seed: int = 0) -> dict:
    arg_keys = jax.random.split(jax.random.key(seed), 19)
    tokens = normal_values(arg_keys[0], (TOKENS, D), 1.0, 6.0, ((0, 32),))
    cotangent = normal_values(arg_keys[1], (TOKENS, D), 1.0, 6.0, ((0, 32),))
    lengths = jax.vmap(lambda own: uneven_parts(own, SEQS, S, MOST, 2))(jax.random.split(arg_keys[2], MICRO)).reshape((MICRO, SEQS)).astype(jnp.int32)
    w_qkv = normal_values(arg_keys[3], (D, 3 * D), D ** -0.5, 0.21875, ((0, 32),), jnp.float32)
    w_out = normal_values(arg_keys[4], (D, D), (D // 32) ** -0.5, 1.25, ((0, 32),), jnp.float32)
    w_fc = normal_values(arg_keys[5], (D, FF), D ** -0.5, 0.21875, ((0, 32),), jnp.float32)
    w_proj = normal_values(arg_keys[6], (FF, D), FF ** -0.5, 0.109375, ((0, 32),), jnp.float32)
    vectors = draw_vectors(jax.random.fold_in(arg_keys[18], 71), 0)
    m_qkv = normal_values(arg_keys[8], (D, 3 * D), (0.11 * PARAMS ** -0.5), 0.00016527923, ((0, 32),), jnp.float32)
    m_out = normal_values(arg_keys[9], (D, D), (0.11 * PARAMS ** -0.5), 0.00016527923, ((0, 32),), jnp.float32)
    m_fc = normal_values(arg_keys[10], (D, FF), (0.11 * PARAMS ** -0.5), 0.00016527923, ((0, 32),), jnp.float32)
    m_proj = normal_values(arg_keys[11], (FF, D), (0.11 * PARAMS ** -0.5), 0.00016527923, ((0, 32),), jnp.float32)
    m_vectors = normal_values(arg_keys[12], (NVEC,), (0.11 * PARAMS ** -0.5), 0.00016527923, ((0, 32),), jnp.float32)
    s_qkv = jnp.clip(jnp.exp(math.log(5.644054112963204e-10) - 1.3862944 * jax.random.uniform(arg_keys[13], (D, 3 * D), jnp.float32) ** block_scale(arg_keys[13], (D, 3 * D), ((0, 32),), -0.2, 0.2)), 1.411013528240801e-10, 5.644054112963204e-10)
    s_out = jnp.clip(jnp.exp(math.log(5.644054112963204e-10) - 1.3862944 * jax.random.uniform(arg_keys[14], (D, D), jnp.float32) ** block_scale(arg_keys[14], (D, D), ((0, 32),), -0.2, 0.2)), 1.411013528240801e-10, 5.644054112963204e-10)
    s_fc = jnp.clip(jnp.exp(math.log(5.644054112963204e-10) - 1.3862944 * jax.random.uniform(arg_keys[15], (D, FF), jnp.float32) ** block_scale(arg_keys[15], (D, FF), ((0, 32),), -0.2, 0.2)), 1.411013528240801e-10, 5.644054112963204e-10)
    s_proj = jnp.clip(jnp.exp(math.log(5.644054112963204e-10) - 1.3862944 * jax.random.uniform(arg_keys[16], (FF, D), jnp.float32) ** block_scale(arg_keys[16], (FF, D), ((0, 32),), -0.2, 0.2)), 1.411013528240801e-10, 5.644054112963204e-10)
    s_vectors = jnp.clip(jnp.exp(math.log(5.644054112963204e-10) - 1.3862944 * jax.random.uniform(arg_keys[17], (NVEC,), jnp.float32) ** block_scale(arg_keys[17], (NVEC,), ((0, 32),), -0.2, 0.2)), 1.411013528240801e-10, 5.644054112963204e-10)
    return {"tokens": tokens, "cotangent": cotangent, "lengths": lengths, "w_qkv": w_qkv, "w_out": w_out, "w_fc": w_fc, "w_proj": w_proj, "vectors": vectors, "m_qkv": m_qkv, "m_out": m_out, "m_fc": m_fc, "m_proj": m_proj, "m_vectors": m_vectors, "s_qkv": s_qkv, "s_out": s_out, "s_fc": s_fc, "s_proj": s_proj, "s_vectors": s_vectors}


HIGHEST = lax.Precision.HIGHEST
EPS_NORM = 1e-05
THRESH = 1.0
BETA_ONE = 0.9
BETA_TWO = 0.999
LR_MAT = 0.03
LR_VEC = 0.5
WEIGHT_DECAY = 0.1
EPS_ADAM = 1e-08
BIG_NEG = -1e+30

@jax.custom_vjp
def low(v):
    return lax.optimization_barrier(v.astype(jnp.bfloat16)).astype(jnp.float32)

@jax.custom_vjp
def low_back(v):
    return v

def low_keep(v):
    return (low(v), None)

def low_pass(kept, grad):
    return (grad,)

def back_keep(v):
    return (v, None)

def back_low(kept, grad):
    return (low(grad),)
low.defvjp(low_keep, low_pass)
low_back.defvjp(back_keep, back_low)

def segment_ids(lengths_row, extent):
    ends_all = jnp.cumsum(lengths_row).astype(jnp.int32)
    places = jnp.arange(extent, dtype=jnp.int32)
    return lax.optimization_barrier(jnp.sum((places[:, None] >= ends_all[None, :]).astype(jnp.int32), axis=1)).astype(jnp.int32)

def norm_rows(values_in, scaling, offset):
    center = values_in - lax.optimization_barrier(jnp.mean(values_in, axis=-1, keepdims=True))
    variance = lax.optimization_barrier(jnp.mean(center * center, axis=-1, keepdims=True))
    return center * lax.rsqrt(variance + EPS_NORM) * scaling + offset

def split_vectors(vec_all):
    pieces = [vec_all[position * D:(position + 1) * D] for position in range(8)]
    return pieces + [vec_all[8 * D:]]

def attend(queries, keys_all, values_all, segment):
    extent = queries.shape[0]
    places = jnp.arange(extent, dtype=jnp.int32)
    allowed = (segment[:, None] == segment[None, :]) & (places[:, None] >= places[None, :])
    scores = jnp.einsum('qhd,khd->hqk', queries, keys_all, precision=HIGHEST) * HD ** (-0.5)
    scores = low_back(scores)
    scores = jnp.where(allowed[None], scores, BIG_NEG)
    highest = lax.optimization_barrier(jnp.max(scores, axis=-1, keepdims=True))
    exponent = jnp.exp(scores - highest)
    soft_probs = exponent / lax.optimization_barrier(jnp.sum(exponent, axis=-1, keepdims=True))
    return jnp.einsum('hqk,khd->qhd', low(soft_probs), values_all, precision=HIGHEST)

def layer_step(rounded, inputs, segment):
    low_qkv, low_out, low_fc, low_proj, low_vec = rounded
    gain_one, bias_one, bias_query, bias_value, bias_out, gain_two, bias_two, bias_proj, bias_fc = split_vectors(low_vec)
    extent = inputs.shape[0]
    normed_one = low(norm_rows(inputs, gain_one, bias_one))
    bias_mixed = jnp.concatenate([bias_query, jnp.zeros_like(bias_query), bias_value])
    mixed_qkv = jnp.dot(normed_one, low_qkv, precision=HIGHEST) + bias_mixed
    mixed_qkv = low(low_back(mixed_qkv))
    queries = mixed_qkv[:, :D].reshape(extent, H, HD)
    keys_all = mixed_qkv[:, D:2 * D].reshape(extent, H, HD)
    values_all = mixed_qkv[:, 2 * D:].reshape(extent, H, HD)
    attended = attend(queries, keys_all, values_all, segment).reshape(extent, D)
    attended = low(low_back(attended))
    branch_one = low_back(jnp.dot(attended, low_out, precision=HIGHEST) + bias_out)
    middle = inputs + branch_one
    normed_two = low(norm_rows(middle, gain_two, bias_two))
    hidden_pre = low_back(jnp.dot(normed_two, low_fc, precision=HIGHEST) + bias_fc)
    activated = low(jax.nn.gelu(hidden_pre, approximate=True))
    branch_two = low_back(jnp.dot(activated, low_proj, precision=HIGHEST) + bias_proj)
    return middle + branch_two

def whole_layer(params, inputs_all, segments):
    rounded = tuple((low(weight) for weight in params))
    runner = jax.checkpoint(layer_step)

    def visit_one(carried, entry_pair):
        return (carried, runner(rounded, entry_pair[0], entry_pair[1]))
    _, outputs = lax.scan(visit_one, jnp.zeros((), jnp.float32), (inputs_all, segments))
    return outputs

def adamw_update(weight, moment_one, moment_two, gradient, step_rate, decay_rate):
    first_new = BETA_ONE * moment_one + (1.0 - BETA_ONE) * gradient
    second_new = BETA_TWO * moment_two + (1.0 - BETA_TWO) * gradient * gradient
    first_hat = first_new / (1.0 - BETA_ONE ** STEP)
    second_hat = second_new / (1.0 - BETA_TWO ** STEP)
    weight_new = weight - step_rate * (first_hat / (jnp.sqrt(second_hat) + EPS_ADAM) + decay_rate * weight)
    return (weight_new, first_new, second_new)

def reference(tokens, cotangent, lengths, w_qkv, w_out, w_fc, w_proj, vectors, m_qkv, m_out, m_fc, m_proj, m_vectors, s_qkv, s_out, s_fc, s_proj, s_vectors):
    params = (w_qkv, w_out, w_fc, w_proj, vectors)
    inputs_all = tokens.astype(jnp.float32).reshape(MICRO, S, D)
    upstream = cotangent.astype(jnp.float32).reshape(MICRO, S, D)
    segments = jax.vmap(lambda r: segment_ids(r, S))(lengths)

    def forward_all(params_in, inputs_in):
        return whole_layer(params_in, inputs_in, segments)
    result, pullback = jax.vjp(forward_all, params, inputs_all)
    grad_params, grad_inputs = pullback(upstream)
    squares = jnp.zeros((), jnp.float32)
    for gradient in grad_params:
        squares = squares + jnp.sum(gradient * gradient)
    norm_total = jnp.sqrt(squares)
    factor = THRESH / jnp.maximum(norm_total, THRESH)
    firsts = (m_qkv, m_out, m_fc, m_proj, m_vectors)
    seconds = (s_qkv, s_out, s_fc, s_proj, s_vectors)
    new_weights = []
    new_firsts = []
    new_seconds = []
    for position in range(5):
        is_vector = position == 4
        step_rate = LR_VEC if is_vector else LR_MAT
        decay_rate = 0.0 if is_vector else WEIGHT_DECAY
        weight_new, first_new, second_new = adamw_update(params[position], firsts[position], seconds[position], grad_params[position] * factor, step_rate, decay_rate)
        new_weights.append(weight_new)
        new_firsts.append(first_new)
        new_seconds.append(second_new)
    output = result.reshape(TOKENS, D).astype(jnp.bfloat16)
    input_grad = grad_inputs.reshape(TOKENS, D)
    return (output, input_grad, norm_total, new_weights[0], new_weights[1], new_weights[2], new_weights[3], new_weights[4], new_firsts[0], new_firsts[1], new_firsts[2], new_firsts[3], new_firsts[4], new_seconds[0], new_seconds[1], new_seconds[2], new_seconds[3], new_seconds[4])
```

```python
import jax
import jax.numpy as jnp
from jax import lax
from jax.sharding import PartitionSpec as P

D = 768
H = 12
HD = 64
STEP = 10


EPS_NORM = 1e-05
THRESH = 1.0
BETA_ONE = 0.9
BETA_TWO = 0.999
LR_MAT = 0.03
LR_VEC = 0.5
WEIGHT_DECAY = 0.1
EPS_ADAM = 1e-08
BIG_NEG = -1e30


def segment_ids(lengths_row, extent):
    ends_all = jnp.cumsum(lengths_row)
    places = jnp.arange(extent, dtype=jnp.int32)
    return jnp.sum((places[:, None] >= ends_all[None, :]).astype(jnp.int32), axis=1)


def norm_rows(values_in, scaling, offset):
    center = values_in - jnp.mean(values_in, axis=-1, keepdims=True)
    variance = jnp.mean(center * center, axis=-1, keepdims=True)
    return center * lax.rsqrt(variance + EPS_NORM) * scaling + offset


def split_vectors(vec_all):
    pieces = [vec_all[position * D : (position + 1) * D] for position in range(8)]
    return pieces + [vec_all[8 * D :]]


def gelu_tanh(z):
    return jax.nn.gelu(z, approximate=True)


def block_mask(segment, start, block_rows, columns):
    rows_here = start + jnp.arange(block_rows, dtype=jnp.int32)
    return (segment[:, None] == segment[None, :]) & (rows_here[:, None] >= columns[None, :])


def attend_forward(queries, keys_all, values_all, segment):
    allowed = block_mask(segment, 0, segment.shape[0], jnp.arange(segment.shape[0]))
    scores = (
        jnp.einsum("qhd,khd->hqk", queries, keys_all, preferred_element_type=jnp.float32)
        * HD ** (-0.5)
    )
    scores = jnp.where(allowed[None], scores, BIG_NEG)
    highest = jnp.max(scores, axis=-1, keepdims=True)
    exponent = jnp.exp(scores - highest)
    totals = jnp.sum(exponent, axis=-1, keepdims=True)
    soft_probs = (exponent / totals).astype(jnp.bfloat16)
    attended = jnp.einsum(
        "hqk,khd->qhd", soft_probs, values_all, preferred_element_type=jnp.float32
    )
    return (attended.reshape(-1, D).astype(jnp.bfloat16), highest + jnp.log(totals))


def attend_backward(queries, keys_all, values_all, grad_rows, log_rows, segment):
    score_scale = HD ** (-0.5)
    allowed = block_mask(segment, 0, segment.shape[0], jnp.arange(segment.shape[0]))
    scores = (
        jnp.einsum("qhd,khd->hqk", queries, keys_all, preferred_element_type=jnp.float32)
        * score_scale
    )
    soft_probs = jnp.where(allowed[None], jnp.exp(scores - log_rows), 0.0)
    grad_values = jnp.einsum(
        "hqk,qhd->khd",
        soft_probs.astype(jnp.bfloat16),
        grad_rows,
        preferred_element_type=jnp.float32,
    )
    grad_probs = jnp.einsum(
        "qhd,khd->hqk", grad_rows, values_all, preferred_element_type=jnp.float32
    )
    grad_scores = soft_probs * (
        grad_probs - jnp.sum(soft_probs * grad_probs, axis=-1, keepdims=True)
    )
    grad_scores = grad_scores.astype(jnp.bfloat16)
    grad_query = (
        jnp.einsum("hqk,khd->qhd", grad_scores, keys_all, preferred_element_type=jnp.float32)
        * score_scale
    )
    grad_keys = (
        jnp.einsum("hqk,qhd->khd", grad_scores, queries, preferred_element_type=jnp.float32)
        * score_scale
    )
    return jnp.concatenate(
        [grad_query.reshape(-1, D), grad_keys.reshape(-1, D), grad_values.reshape(-1, D)], axis=1
    ).astype(jnp.bfloat16)


def all_attend_forward(mixed_qkv, lengths):
    micro_count = lengths.shape[0]
    extent = mixed_qkv.shape[0] // micro_count
    parts = []
    logs = []
    for index in range(micro_count):
        segment = segment_ids(lengths[index], extent)
        rows = mixed_qkv[index * extent : (index + 1) * extent]
        q, k, v = (rows[:, i * D : (i + 1) * D].reshape(extent, H, HD) for i in range(3))
        part, log_rows = attend_forward(q, k, v, segment)
        parts.append(part)
        logs.append(log_rows)
    return jnp.concatenate(parts, axis=0), logs


def all_attend_backward(mixed_qkv, grad_att, attended, logs, lengths):
    micro_count = lengths.shape[0]
    extent = mixed_qkv.shape[0] // micro_count
    parts = []
    for index in range(micro_count):
        segment = segment_ids(lengths[index], extent)
        rows = mixed_qkv[index * extent : (index + 1) * extent]
        q, k, v = (rows[:, i * D : (i + 1) * D].reshape(extent, H, HD) for i in range(3))
        grads = grad_att[index * extent : (index + 1) * extent].reshape(extent, H, HD)
        parts.append(attend_backward(q, k, v, grads, logs[index], segment))
    return jnp.concatenate(parts, axis=0)


def flip_pairs(count, bit):
    return [(place, place ^ (1 << bit)) for place in range(count)]


def spread_orders(count):
    far = list(range(count.bit_length() - 2, 0, -1))
    swapped = far[:-2] + far[-2:][::-1]
    moved = far[:1] + far[2:] + far[1:2]
    return far + [0], swapped + [0], moved + [0]


def gather_rows(piece, order, count):
    me = lax.axis_index("fsdp")
    held = []
    current = piece
    for bit in order:
        other = lax.ppermute(current, "fsdp", flip_pairs(count, bit))
        axis = sum(1 for known in held if known > bit)
        mine_high = ((me >> bit) & 1) == 1
        low = jnp.where(mine_high, other, current)
        high = jnp.where(mine_high, current, other)
        current = jnp.stack([low, high], axis=axis)
        held.append(bit)
    return current.reshape((count * piece.shape[0],) + piece.shape[1:])


class RowSum:
    def __init__(self, total, order, count, kind):
        rows = total.shape[0] // count
        self.bits = list(range(count.bit_length() - 2, -1, -1))
        self.current = total.reshape((2,) * len(self.bits) + (rows,) + total.shape[1:])
        self.order = list(order)
        self.count = count
        self.kind = kind

    def first_send(self):
        return self.half(self.order[0], 1).astype(self.kind)

    def half(self, bit, flipped):
        mine = ((lax.axis_index("fsdp") >> bit) & 1) ^ flipped
        return lax.dynamic_index_in_dim(
            self.current, mine, axis=self.bits.index(bit), keepdims=False
        )

    def finish(self, sent):
        for position, bit in enumerate(self.order):
            if position > 0:
                sent = self.half(bit, 1).astype(self.kind)
            arrived = lax.ppermute(sent, "fsdp", flip_pairs(self.count, bit))
            self.current = self.half(bit, 0) + arrived.astype(jnp.float32)
            self.bits.remove(bit)
        return self.current


def sum_all(value, count):
    total = jnp.full((8, 128), value, jnp.float32)
    for bit in range(count.bit_length() - 1):
        total = total + lax.ppermute(total, "fsdp", flip_pairs(count, bit))
    return total[0, 0]


def adamw_update(weight, moment_one, moment_two, gradient, step_rate, decay_rate):
    first_new = BETA_ONE * moment_one + (1.0 - BETA_ONE) * gradient
    second_new = BETA_TWO * moment_two + (1.0 - BETA_TWO) * gradient * gradient
    first_hat = first_new / (1.0 - BETA_ONE**STEP)
    second_hat = second_new / (1.0 - BETA_TWO**STEP)
    weight_new = weight - step_rate * (
        first_hat / (jnp.sqrt(second_hat) + EPS_ADAM) + decay_rate * weight
    )
    return (weight_new, first_new, second_new)


def per_device(
    tokens,
    cotangent,
    lengths,
    w_qkv,
    w_out,
    w_fc,
    w_proj,
    vectors,
    m_qkv,
    m_out,
    m_fc,
    m_proj,
    m_vectors,
    s_qkv,
    s_out,
    s_fc,
    s_proj,
    s_vectors,
):
    count = lax.axis_size("fsdp")
    order_one, order_two, order_three = spread_orders(count)
    low_vec = gather_rows(vectors.astype(jnp.bfloat16).reshape(1, -1), order_one, count)
    wide_qkv = gather_rows(w_qkv.astype(jnp.bfloat16), order_one, count)
    wide_out = gather_rows(w_out.astype(jnp.bfloat16), order_two, count)
    wide_fc = gather_rows(w_fc.astype(jnp.bfloat16), order_two, count)
    wide_proj = gather_rows(w_proj.astype(jnp.bfloat16), order_three, count)
    gain_one, bias_one, bias_query, bias_value, bias_out, gain_two, bias_two, bias_proj, bias_fc = (
        split_vectors(low_vec.reshape(-1).astype(jnp.float32))
    )
    inputs = tokens.astype(jnp.float32)
    normed_one = norm_rows(inputs, gain_one, bias_one).astype(jnp.bfloat16)
    bias_mixed = jnp.concatenate([bias_query, jnp.zeros_like(bias_query), bias_value])
    mixed_qkv = (
        jnp.dot(normed_one, wide_qkv, preferred_element_type=jnp.float32) + bias_mixed
    ).astype(jnp.bfloat16)
    attended, logs = all_attend_forward(mixed_qkv, lengths)
    middle = inputs + jnp.dot(attended, wide_out, preferred_element_type=jnp.float32) + bias_out
    normed_two = norm_rows(middle, gain_two, bias_two).astype(jnp.bfloat16)
    hidden_pre = jnp.dot(normed_two, wide_fc, preferred_element_type=jnp.float32) + bias_fc
    activated = gelu_tanh(hidden_pre).astype(jnp.bfloat16)

    upstream = cotangent.astype(jnp.float32)
    grad_proj = jnp.einsum("tf,td->fd", activated, cotangent, preferred_element_type=jnp.float32)
    sum_proj = RowSum(grad_proj, order_three[::-1], count, jnp.bfloat16)
    send_proj = sum_proj.first_send()
    grad_act = jnp.einsum("td,fd->tf", cotangent, wide_proj, preferred_element_type=jnp.float32)
    _, gelu_back = jax.vjp(gelu_tanh, hidden_pre)
    grad_pre = gelu_back(grad_act)[0].astype(jnp.bfloat16)
    grad_pre, send_proj = lax.optimization_barrier((grad_pre, send_proj))
    result = middle + jnp.dot(activated, wide_proj, preferred_element_type=jnp.float32) + bias_proj
    output = result.astype(jnp.bfloat16)
    grad_fc = jnp.einsum("td,tf->df", normed_two, grad_pre, preferred_element_type=jnp.float32)
    sum_fc = RowSum(grad_fc, order_two[::-1], count, jnp.bfloat16)
    send_fc = sum_fc.first_send()
    grad_normed_two = jnp.einsum("tf,df->td", grad_pre, wide_fc, preferred_element_type=jnp.float32)
    _, norm_back_two = jax.vjp(norm_rows, middle, gain_two, bias_two)
    grad_middle_part, grad_gain_two, grad_bias_two = norm_back_two(grad_normed_two)
    grad_middle = upstream + grad_middle_part
    grad_one = grad_middle.astype(jnp.bfloat16)
    grad_out = jnp.einsum("te,td->ed", attended, grad_one, preferred_element_type=jnp.float32)
    sum_out = RowSum(grad_out, order_one[::-1], count, jnp.bfloat16)
    send_out = sum_out.first_send()
    grad_att = jnp.einsum(
        "td,ed->te", grad_one, wide_out, preferred_element_type=jnp.float32
    ).astype(jnp.bfloat16)
    grad_att, send_fc, send_out = lax.optimization_barrier((grad_att, send_fc, send_out))
    grad_mixed = all_attend_backward(mixed_qkv, grad_att, attended, logs, lengths)
    grad_qkv = jnp.einsum("td,te->de", normed_one, grad_mixed, preferred_element_type=jnp.float32)
    width = grad_qkv.shape[1] // 2
    sum_left = RowSum(grad_qkv[:, :width], order_one[::-1], count, jnp.bfloat16)
    sum_right = RowSum(grad_qkv[:, width:], order_two[::-1], count, jnp.bfloat16)
    send_left = sum_left.first_send()
    send_right = sum_right.first_send()
    grad_mixed, send_left, send_right = lax.optimization_barrier(
        (grad_mixed, send_left, send_right)
    )
    grad_normed_one = jnp.einsum(
        "te,de->td", grad_mixed, wide_qkv, preferred_element_type=jnp.float32
    )
    _, norm_back_one = jax.vjp(norm_rows, inputs, gain_one, bias_one)
    grad_in_part, grad_gain_one, grad_bias_one = norm_back_one(grad_normed_one)
    input_grad = grad_middle + grad_in_part
    grad_bias_mixed = jnp.sum(grad_mixed.astype(jnp.float32), axis=0)
    grad_vec = jnp.concatenate(
        [
            grad_gain_one,
            grad_bias_one,
            grad_bias_mixed[:D],
            grad_bias_mixed[2 * D :],
            jnp.sum(grad_one.astype(jnp.float32), axis=0),
            grad_gain_two,
            grad_bias_two,
            jnp.sum(upstream, axis=0),
            jnp.sum(grad_pre.astype(jnp.float32), axis=0),
        ]
    )
    sum_vec = RowSum(grad_vec.reshape(count, -1), order_one[::-1], count, jnp.float32)
    owned_proj = sum_proj.finish(send_proj)
    owned_fc = sum_fc.finish(send_fc)
    owned_out = sum_out.finish(send_out)
    owned_qkv = jnp.concatenate(
        [sum_left.finish(send_left), sum_right.finish(send_right)], axis=1
    )
    owned_vec = sum_vec.finish(sum_vec.first_send()).reshape(-1)
    owned = (owned_qkv, owned_out, owned_fc, owned_proj, owned_vec)
    local_sum = jnp.zeros((), jnp.float32)
    for gradient in owned:
        local_sum = local_sum + jnp.sum(gradient * gradient)
    norm_total = jnp.sqrt(sum_all(local_sum, count))
    factor = THRESH / jnp.maximum(norm_total, THRESH)
    params = (w_qkv, w_out, w_fc, w_proj, vectors)
    firsts = (m_qkv, m_out, m_fc, m_proj, m_vectors)
    seconds = (s_qkv, s_out, s_fc, s_proj, s_vectors)
    new_weights = []
    new_firsts = []
    new_seconds = []
    for position in range(5):
        is_vector = position == 4
        step_rate = LR_VEC if is_vector else LR_MAT
        decay_rate = 0.0 if is_vector else WEIGHT_DECAY
        weight_new, first_new, second_new = adamw_update(
            params[position],
            firsts[position],
            seconds[position],
            owned[position] * factor,
            step_rate,
            decay_rate,
        )
        new_weights.append(weight_new)
        new_firsts.append(first_new)
        new_seconds.append(second_new)
    return (
        output,
        input_grad,
        norm_total,
        new_weights[0],
        new_weights[1],
        new_weights[2],
        new_weights[3],
        new_weights[4],
        new_firsts[0],
        new_firsts[1],
        new_firsts[2],
        new_firsts[3],
        new_firsts[4],
        new_seconds[0],
        new_seconds[1],
        new_seconds[2],
        new_seconds[3],
        new_seconds[4],
    )


def solution(mesh):
    in_specs = (
        P("fsdp", None),
        P("fsdp", None),
        P("fsdp", None),
        P("fsdp", None),
        P("fsdp", None),
        P("fsdp", None),
        P("fsdp", None),
        P("fsdp"),
        P("fsdp", None),
        P("fsdp", None),
        P("fsdp", None),
        P("fsdp", None),
        P("fsdp"),
        P("fsdp", None),
        P("fsdp", None),
        P("fsdp", None),
        P("fsdp", None),
        P("fsdp"),
    )
    out_specs = (
        P("fsdp", None),
        P("fsdp", None),
        P(),
        P("fsdp", None),
        P("fsdp", None),
        P("fsdp", None),
        P("fsdp", None),
        P("fsdp"),
        P("fsdp", None),
        P("fsdp", None),
        P("fsdp", None),
        P("fsdp", None),
        P("fsdp"),
        P("fsdp", None),
        P("fsdp", None),
        P("fsdp", None),
        P("fsdp", None),
        P("fsdp"),
    )
    return jax.shard_map(
        per_device, mesh=mesh, in_specs=in_specs, out_specs=out_specs, check_vma=False
    )
```

```python
import jax
import jax.numpy as jnp
from jax import lax
from jax.experimental import pallas as pl
from jax.experimental.pallas import tpu as pltpu
from jax.sharding import PartitionSpec as P

D = 768
H = 12
HD = 64
STEP = 10


EPS_NORM = 1e-05
THRESH = 1.0
BETA_ONE = 0.9
BETA_TWO = 0.999
LR_MAT = 0.03
LR_VEC = 0.5
WEIGHT_DECAY = 0.1
EPS_ADAM = 1e-08
BIG_NEG = -1e30


def segment_ids(lengths_row, extent):
    ends_all = jnp.cumsum(lengths_row)
    places = jnp.arange(extent, dtype=jnp.int32)
    return jnp.sum((places[:, None] >= ends_all[None, :]).astype(jnp.int32), axis=1)


def norm_rows(values_in, scaling, offset):
    center = values_in - jnp.mean(values_in, axis=-1, keepdims=True)
    variance = jnp.mean(center * center, axis=-1, keepdims=True)
    return center * lax.rsqrt(variance + EPS_NORM) * scaling + offset


def split_vectors(vec_all):
    pieces = [vec_all[position * D : (position + 1) * D] for position in range(8)]
    return pieces + [vec_all[8 * D :]]


def gelu_tanh(z):
    return jax.nn.gelu(z, approximate=True)


def head_probs(queries, keys, allowed):
    scores = lax.dot_general(
        queries, keys, (((1,), (1,)), ((), ())), preferred_element_type=jnp.float32
    )
    scores = jnp.where(allowed, scores * HD ** (-0.5), BIG_NEG)
    exponent = jnp.exp(scores - jnp.max(scores, axis=-1, keepdims=True))
    return exponent * (1.0 / jnp.sum(exponent, axis=-1, keepdims=True))


def allowed_pairs(column_ref, row_ref):
    extent = column_ref.shape[0]
    places = lax.broadcasted_iota(jnp.int32, (extent, extent), 0)
    others = lax.broadcasted_iota(jnp.int32, (extent, extent), 1)
    return (column_ref[...] == row_ref[0]) & (places >= others)


def forward_kernel(q_ref, k_ref, v_ref, column_ref, row_ref, out_ref):
    allowed = allowed_pairs(column_ref, row_ref)
    for start in range(0, q_ref.shape[1], HD):
        head = slice(start, start + HD)
        probs = head_probs(q_ref[:, head], k_ref[:, head], allowed).astype(jnp.bfloat16)
        out_ref[:, head] = jnp.dot(
            probs, v_ref[:, head], preferred_element_type=jnp.float32
        ).astype(jnp.bfloat16)


def backward_kernel(q_ref, k_ref, v_ref, grad_ref, column_ref, row_ref, out_ref):
    allowed = allowed_pairs(column_ref, row_ref)
    scale = HD ** (-0.5)
    across = (((0,), (0,)), ((), ()))
    for start in range(0, q_ref.shape[1], HD):
        head = slice(start, start + HD)
        queries, keys, values, grads = (
            ref[:, head] for ref in (q_ref, k_ref, v_ref, grad_ref)
        )
        probs = head_probs(queries, keys, allowed)
        grad_probs = lax.dot_general(
            grads, values, (((1,), (1,)), ((), ())), preferred_element_type=jnp.float32
        )
        inner = jnp.sum(probs * grad_probs, axis=-1, keepdims=True)
        grad_scores = (probs * (grad_probs - inner)).astype(jnp.bfloat16)
        grad_values = lax.dot_general(
            probs.astype(jnp.bfloat16), grads, across, preferred_element_type=jnp.float32
        )
        grad_query = jnp.dot(grad_scores, keys, preferred_element_type=jnp.float32) * scale
        grad_keys = (
            lax.dot_general(grad_scores, queries, across, preferred_element_type=jnp.float32)
            * scale
        )
        out_ref[0, :, head] = grad_query.astype(jnp.bfloat16)
        out_ref[1, :, head] = grad_keys.astype(jnp.bfloat16)
        out_ref[2, :, head] = grad_values.astype(jnp.bfloat16)


def attend(mixed_qkv, segments, grad_att=None):
    micro_count, extent = segments.shape
    wide = 2 * HD
    blocks = D // wide
    row = lambda shift: pl.BlockSpec((extent, wide), lambda m, h: (m, h + shift))
    in_specs = [row(0), row(blocks), row(2 * blocks)]
    operands = [mixed_qkv] * 3
    tokens_here = mixed_qkv.shape[0]
    if grad_att is None:
        kernel, dots = forward_kernel, 2
        out_shape = jax.ShapeDtypeStruct((tokens_here, D), jnp.bfloat16)
        out_spec = row(0)
    else:
        kernel, dots = backward_kernel, 5
        in_specs.append(row(0))
        operands.append(grad_att)
        out_shape = jax.ShapeDtypeStruct((3, tokens_here, D), jnp.bfloat16)
        out_spec = pl.BlockSpec((3, extent, wide), lambda m, h: (0, m, h))
    in_specs.append(pl.BlockSpec((extent, 1), lambda m, h: (m, 0)))
    in_specs.append(pl.BlockSpec((1, 1, extent), lambda m, h: (m, 0, 0)))
    operands += [segments.reshape(-1, 1), segments.reshape(micro_count, 1, extent)]
    area = tokens_here * extent * H
    return pl.pallas_call(
        kernel,
        grid=(micro_count, blocks),
        in_specs=in_specs,
        out_specs=out_spec,
        out_shape=out_shape,
        cost_estimate=pl.CostEstimate(
            flops=2 * dots * area * HD, bytes_accessed=8 * tokens_here * D, transcendentals=area
        ),
        compiler_params=pltpu.CompilerParams(vmem_limit_bytes=40 * 1024 * 1024),
    )(*operands)


def flip_pairs(count, bit):
    return [(place, place ^ (1 << bit)) for place in range(count)]


def spread_orders(count):
    far = list(range(count.bit_length() - 2, 0, -1))
    swapped = far[:-2] + far[-2:][::-1]
    moved = far[:1] + far[2:] + far[1:2]
    return far + [0], swapped + [0], moved + [0]


def gather_rows(piece, order, count):
    me = lax.axis_index("fsdp")
    held = []
    current = piece
    for bit in order:
        other = lax.ppermute(current, "fsdp", flip_pairs(count, bit))
        axis = sum(1 for known in held if known > bit)
        mine_high = ((me >> bit) & 1) == 1
        low = jnp.where(mine_high, other, current)
        high = jnp.where(mine_high, current, other)
        current = jnp.stack([low, high], axis=axis)
        held.append(bit)
    return current.reshape((count * piece.shape[0],) + piece.shape[1:])


class RowSum:
    def __init__(self, total, order, count, kind):
        rows = total.shape[0] // count
        self.bits = list(range(count.bit_length() - 2, -1, -1))
        self.current = total.reshape((2,) * len(self.bits) + (rows,) + total.shape[1:])
        self.order = list(order)
        self.count = count
        self.kind = kind
        self.prepare()

    def half(self, bit, flipped):
        mine = ((lax.axis_index("fsdp") >> bit) & 1) ^ flipped
        return lax.dynamic_index_in_dim(
            self.current, mine, axis=self.bits.index(bit), keepdims=False
        )

    def prepare(self):
        if self.order:
            self.sent = self.half(self.order[0], 1).astype(self.kind)
            self.kept = self.half(self.order[0], 0)

    def step(self):
        if self.order:
            bit = self.order.pop(0)
            arrived = lax.ppermute(self.sent, "fsdp", flip_pairs(self.count, bit))
            self.current = self.kept + arrived.astype(jnp.float32)
            self.bits.remove(bit)
            self.prepare()

    def finish(self):
        while self.order:
            self.step()
        return self.current


def step_all(sums):
    for part in sums:
        part.step()


def tie(value, sums):
    sums = [part for part in sums if part.order]
    value, sent = lax.optimization_barrier((value, [part.sent for part in sums]))
    for part, piece in zip(sums, sent):
        part.sent = piece
    return value


def sum_all(value, count):
    total = jnp.full((8, 128), value, jnp.float32)
    for bit in range(count.bit_length() - 1):
        total = total + lax.ppermute(total, "fsdp", flip_pairs(count, bit))
    return total[0, 0]


def adamw_update(weight, moment_one, moment_two, gradient, step_rate, decay_rate):
    first_new = BETA_ONE * moment_one + (1.0 - BETA_ONE) * gradient
    second_new = BETA_TWO * moment_two + (1.0 - BETA_TWO) * gradient * gradient
    first_hat = first_new / (1.0 - BETA_ONE**STEP)
    second_hat = second_new / (1.0 - BETA_TWO**STEP)
    weight_new = weight - step_rate * (
        first_hat / (jnp.sqrt(second_hat) + EPS_ADAM) + decay_rate * weight
    )
    return (weight_new, first_new, second_new)


def per_device(
    tokens,
    cotangent,
    lengths,
    w_qkv,
    w_out,
    w_fc,
    w_proj,
    vectors,
    m_qkv,
    m_out,
    m_fc,
    m_proj,
    m_vectors,
    s_qkv,
    s_out,
    s_fc,
    s_proj,
    s_vectors,
):
    count = lax.axis_size("fsdp")
    order_one, order_two, order_three = spread_orders(count)
    low_vec = gather_rows(vectors.astype(jnp.bfloat16).reshape(1, -1), order_one, count)
    wide_qkv = gather_rows(w_qkv.astype(jnp.bfloat16), order_one, count)
    wide_out = gather_rows(w_out.astype(jnp.bfloat16), order_two, count)
    wide_fc = gather_rows(w_fc.astype(jnp.bfloat16), order_two, count)
    wide_proj = gather_rows(w_proj.astype(jnp.bfloat16), order_three, count)
    gain_one, bias_one, bias_query, bias_value, bias_out, gain_two, bias_two, bias_proj, bias_fc = (
        split_vectors(low_vec.reshape(-1).astype(jnp.float32))
    )
    inputs = tokens.astype(jnp.float32)
    normed_one = norm_rows(inputs, gain_one, bias_one).astype(jnp.bfloat16)
    bias_mixed = jnp.concatenate([bias_query, jnp.zeros_like(bias_query), bias_value])
    mixed_qkv = (
        jnp.dot(normed_one, wide_qkv, preferred_element_type=jnp.float32) + bias_mixed
    ).astype(jnp.bfloat16)
    extent = tokens.shape[0] // lengths.shape[0]
    segments = jnp.stack([segment_ids(lengths[i], extent) for i in range(lengths.shape[0])])
    attended = attend(mixed_qkv, segments)
    middle = inputs + jnp.dot(attended, wide_out, preferred_element_type=jnp.float32) + bias_out
    normed_two = norm_rows(middle, gain_two, bias_two).astype(jnp.bfloat16)
    hidden_pre = jnp.dot(normed_two, wide_fc, preferred_element_type=jnp.float32) + bias_fc
    activated = gelu_tanh(hidden_pre).astype(jnp.bfloat16)

    upstream = cotangent.astype(jnp.float32)
    grad_proj = jnp.einsum("tf,td->fd", activated, cotangent, preferred_element_type=jnp.float32)
    sum_proj = RowSum(grad_proj, order_three[::-1], count, jnp.bfloat16)
    grad_act = jnp.einsum("td,fd->tf", cotangent, wide_proj, preferred_element_type=jnp.float32)
    _, gelu_back = jax.vjp(gelu_tanh, hidden_pre)
    grad_pre = gelu_back(grad_act)[0].astype(jnp.bfloat16)
    grad_pre = tie(grad_pre, [sum_proj])
    grad_fc = jnp.einsum("td,tf->df", normed_two, grad_pre, preferred_element_type=jnp.float32)
    sum_fc = RowSum(grad_fc, order_two[::-1], count, jnp.bfloat16)
    sum_proj.step()
    grad_normed_two = jnp.einsum("tf,df->td", grad_pre, wide_fc, preferred_element_type=jnp.float32)
    grad_normed_two = tie(grad_normed_two, [sum_proj, sum_fc])
    _, norm_back_two = jax.vjp(norm_rows, middle, gain_two, bias_two)
    grad_middle_part, grad_gain_two, grad_bias_two = norm_back_two(grad_normed_two)
    grad_middle = upstream + grad_middle_part
    grad_one = grad_middle.astype(jnp.bfloat16)
    grad_out = jnp.einsum("te,td->ed", attended, grad_one, preferred_element_type=jnp.float32)
    sum_out = RowSum(grad_out, order_one[::-1], count, jnp.bfloat16)
    grad_att = jnp.einsum(
        "td,ed->te", grad_one, wide_out, preferred_element_type=jnp.float32
    ).astype(jnp.bfloat16)
    sum_fc.step()
    grad_att = tie(grad_att, [sum_proj, sum_fc, sum_out])
    grad_mixed = attend(mixed_qkv, segments, grad_att)
    early = [sum_proj, sum_fc, sum_out]
    step_all(early)
    grad_mixed = tie(grad_mixed, early)
    orders = (order_one, order_two, order_three)
    late = []
    for index in range(3):
        grad_part = jnp.einsum(
            "td,te->de", normed_one, grad_mixed[index], preferred_element_type=jnp.float32
        )
        late.append(RowSum(grad_part, orders[index][::-1], count, jnp.bfloat16))
    grad_mixed = tie(grad_mixed, late)
    grad_normed_one = jnp.zeros((), jnp.float32)
    for index in range(3):
        grad_normed_one = grad_normed_one + jnp.einsum(
            "te,de->td",
            grad_mixed[index],
            wide_qkv[:, index * D : (index + 1) * D],
            preferred_element_type=jnp.float32,
        )
    step_all(late)
    step_all(early)
    grad_normed_one = tie(grad_normed_one, late + early)
    _, norm_back_one = jax.vjp(norm_rows, inputs, gain_one, bias_one)
    grad_in_part, grad_gain_one, grad_bias_one = norm_back_one(grad_normed_one)
    input_grad = grad_middle + grad_in_part
    grad_vec = jnp.concatenate(
        [
            grad_gain_one,
            grad_bias_one,
            jnp.sum(grad_mixed[0].astype(jnp.float32), axis=0),
            jnp.sum(grad_mixed[2].astype(jnp.float32), axis=0),
            jnp.sum(grad_one.astype(jnp.float32), axis=0),
            grad_gain_two,
            grad_bias_two,
            jnp.sum(upstream, axis=0),
            jnp.sum(grad_pre.astype(jnp.float32), axis=0),
        ]
    )
    sum_vec = RowSum(grad_vec.reshape(count, -1), order_one[::-1], count, jnp.float32)
    last = late + early + [sum_vec]
    step_all(last)
    result = middle + jnp.dot(activated, wide_proj, preferred_element_type=jnp.float32) + bias_proj
    output = tie(result.astype(jnp.bfloat16), last)
    while any(part.order for part in last):
        step_all(last)
    owned_qkv = jnp.concatenate([part.current for part in late], axis=1)
    owned_out, owned_fc, owned_proj = sum_out.current, sum_fc.current, sum_proj.current
    owned_vec = sum_vec.current.reshape(-1)
    owned = (owned_qkv, owned_out, owned_fc, owned_proj, owned_vec)
    local_sum = jnp.zeros((), jnp.float32)
    for gradient in owned:
        local_sum = local_sum + jnp.sum(gradient * gradient)
    norm_total = jnp.sqrt(sum_all(local_sum, count))
    factor = THRESH / jnp.maximum(norm_total, THRESH)
    params = (w_qkv, w_out, w_fc, w_proj, vectors)
    firsts = (m_qkv, m_out, m_fc, m_proj, m_vectors)
    seconds = (s_qkv, s_out, s_fc, s_proj, s_vectors)
    new_weights = []
    new_firsts = []
    new_seconds = []
    for position in range(5):
        is_vector = position == 4
        step_rate = LR_VEC if is_vector else LR_MAT
        decay_rate = 0.0 if is_vector else WEIGHT_DECAY
        weight_new, first_new, second_new = adamw_update(
            params[position],
            firsts[position],
            seconds[position],
            owned[position] * factor,
            step_rate,
            decay_rate,
        )
        new_weights.append(weight_new)
        new_firsts.append(first_new)
        new_seconds.append(second_new)
    return (
        output,
        input_grad,
        norm_total,
        new_weights[0],
        new_weights[1],
        new_weights[2],
        new_weights[3],
        new_weights[4],
        new_firsts[0],
        new_firsts[1],
        new_firsts[2],
        new_firsts[3],
        new_firsts[4],
        new_seconds[0],
        new_seconds[1],
        new_seconds[2],
        new_seconds[3],
        new_seconds[4],
    )


def solution(mesh):
    in_specs = (
        P("fsdp", None),
        P("fsdp", None),
        P("fsdp", None),
        P("fsdp", None),
        P("fsdp", None),
        P("fsdp", None),
        P("fsdp", None),
        P("fsdp"),
        P("fsdp", None),
        P("fsdp", None),
        P("fsdp", None),
        P("fsdp", None),
        P("fsdp"),
        P("fsdp", None),
        P("fsdp", None),
        P("fsdp", None),
        P("fsdp", None),
        P("fsdp"),
    )
    out_specs = (
        P("fsdp", None),
        P("fsdp", None),
        P(),
        P("fsdp", None),
        P("fsdp", None),
        P("fsdp", None),
        P("fsdp", None),
        P("fsdp"),
        P("fsdp", None),
        P("fsdp", None),
        P("fsdp", None),
        P("fsdp", None),
        P("fsdp"),
        P("fsdp", None),
        P("fsdp", None),
        P("fsdp", None),
        P("fsdp", None),
        P("fsdp"),
    )
    return jax.shard_map(
        per_device, mesh=mesh, in_specs=in_specs, out_specs=out_specs, check_vma=False
    )
```
